32 devices in a mesh: ctx: 4 (over y, x), frame: 8 (over z, core).
Axes of the slice: x: 2, y: 2, z: 4, core: 2. Of those that a mesh axis runs over, the one named last changes fastest.
Arguments:
- queries: bfloat16 [1024, 2048], P('ctx', 'frame'), may hold values from -160 to 160
- keys: bfloat16 [4096, 2048], P('ctx', 'frame'), may hold values from -4 to 4
- values: bfloat16 [4096, 2048], P('ctx', 'frame'), may hold values from -6 to 6
- query_frames: int32 [64], P('ctx'), may hold values from 0 to 191, as said below
- frame_counts: int32 [256], replicated, may hold values from 0 to 16, as said below
- clip_of_frame: int32 [64], P('ctx'), may hold values from 0 to 7, as said below
- in_proj: bfloat16 [2048, 1024], P('frame'), may hold values from -0.125 to 0.125
- mlp_up: bfloat16 [1024, 4096], replicated, may hold values from -0.1875 to 0.1875
- mlp_down: bfloat16 [4096, 1024], replicated, may hold values from -0.09375 to 0.09375
- reward_head: float32 [1024], replicated, may hold values from -0.1875 to 0.1875
Outputs:
- query_grad: float32 [1024, 2048], P('ctx', 'frame')
- key_grad: float32 [4096, 2048], P('ctx', 'frame')
- value_grad: float32 [4096, 2048], P('ctx', 'frame')
- clip_reward: float32 [32], P(('ctx', 'frame'))
The draws below stay inside these ranges and needn't reach their ends.
Inputs may be any that keep to these rules, and one draw needn't show every extreme that they name: `query_frames`: the query patch rows are distinct rows of the first 256 * 3 // 4 patch rows of the video, in increasing order, all of them live; the first and the last of those rows are always among them. `frame_counts`: the live tokens are a prefix of the sequence of at least three quarters of it: rows before the prefix's end are full, one row may be partly live, the rows after it have none, and the last row has none. `clip_of_frame`: within each aligned block of 16 patch row slots every clip number appears exactly 2 times.
All inputs are finite; a program needn't handle non-finite values.
Results may differ from the reference program's by a relative error of at most 0.02.
Values may be sent and summed in bfloat16 or wider, within the bound.
A program may use at most 192 MiB of HBM per device.

```python
import math
import jax
import jax.numpy as jnp
from jax import lax

HD = 128
VD = 1024
VFF = 4096
FTOK = 16
CLIP = 2
HEADS = 16
D = 2048
KTOK = 4096
KFRAMES = 256
QFR_DEV = 16
QTOK = 1024
QFRAMES = 64
NCLIPS = 32
N_FRAME = 8


def draw_keys(key, part):
    return jax.random.truncated_normal(jax.random.fold_in(key, 5), -4.0, 4.0, (KTOK, D), jnp.float32).astype(jnp.bfloat16)


def draw_query_frames(key, part):
    range_rows = KFRAMES * 3 // 4
    order = jax.random.permutation(jax.random.fold_in(key, 41), range_rows - 2)[:QFRAMES - 2] + 1
    inner = jnp.sort(order.astype(jnp.int32))
    first = jnp.zeros((1,), jnp.int32)
    last = jnp.full((1,), range_rows - 1, jnp.int32)
    return jnp.concatenate([first, inner, last]).astype(jnp.int32)


def draw_queries(key, part):
    base_key = jax.random.fold_in(jax.random.fold_in(key, 11), 0)
    base_draw = jax.random.truncated_normal(base_key, -4.0, 4.0, (QTOK, D), jnp.float32)
    result = base_draw
    return result.astype(jnp.bfloat16)


def layout_length(key):
    return jax.random.randint(jax.random.fold_in(key, 37), (), KTOK * 3 // 4, KTOK - FTOK + 1)


def draw_frame_counts(key, part):
    live_length = layout_length(key)
    remain = live_length - jnp.arange(KFRAMES, dtype=jnp.int32) * FTOK
    return jnp.clip(remain, 0, FTOK).astype(jnp.int32)


def draw_clip_of_frame(key, part):
    block_count = QFRAMES // QFR_DEV
    block_keys = jax.random.split(jax.random.fold_in(key, 23), block_count)

    def one_block(block_key):
        return jax.random.permutation(block_key, QFR_DEV)
    orders = jax.vmap(one_block)(block_keys)
    return (orders // CLIP).reshape(-1).astype(jnp.int32)


def levels(key, extent, shards, low, high):
    loudness = 1.0
    for axis_at, blocks in shards:
        steps = jax.random.uniform(jax.random.fold_in(jax.random.fold_in(key, 6), axis_at), (blocks,), jnp.float32, low / len(shards), high / len(shards))
        loudness = loudness * jnp.repeat(jnp.exp(steps), extent[axis_at] // blocks).reshape((-1,) + (1,) * (len(extent) - 1 - axis_at))
    return loudness


def centred(rng, dims, scale, reach, shards=(), kind=jnp.bfloat16):
    loudness = levels(rng, dims, shards, -0.22, 0.18) if shards else 1.0
    values = jax.random.normal(rng, dims, jnp.float32) * scale * loudness
    return jnp.minimum(jnp.maximum(values, -reach), reach).astype(kind)


def setup_inputs(seed: int = 0) -> dict:
    key_of = jax.random.split(jax.random.key(seed), 11)
    queries = draw_queries(jax.random.fold_in(key_of[10], 71), 0)
    keys = draw_keys(jax.random.fold_in(key_of[10], 71), 0)
    values = centred(key_of[2], (KTOK, D), 1.0, 6.0, ((0, 4), (1, 8)))
    query_frames = draw_query_frames(jax.random.fold_in(key_of[10], 71), 0)
    frame_counts = draw_frame_counts(jax.random.fold_in(key_of[10], 71), 0)
    clip_of_frame = draw_clip_of_frame(jax.random.fold_in(key_of[10], 71), 0)
    in_proj = centred(key_of[6], (D, VD), D ** -0.5, 0.125, ((0, 8),))
    mlp_up = centred(key_of[7], (VD, VFF), VD ** -0.5, 0.1875)
    mlp_down = centred(key_of[8], (VFF, VD), VFF ** -0.5, 0.09375)
    reward_head = centred(key_of[9], (VD,), VD ** -0.5, 0.1875, (), jnp.float32)
    return {"queries": queries, "keys": keys, "values": values, "query_frames": query_frames, "frame_counts": frame_counts, "clip_of_frame": clip_of_frame, "in_proj": in_proj, "mlp_up": mlp_up, "mlp_down": mlp_down, "reward_head": reward_head}


EPSILON = 1e-05

def rotate(values_in, position, inverse):
    row_count = values_in.shape[0]
    half_width = HD // 2
    pieces = values_in.reshape(row_count, -1, HD)
    frequency = jnp.exp(-math.log(10000.0) * jnp.arange(half_width, dtype=jnp.float32) / half_width)
    angle = position.astype(jnp.float32)[:, None] * frequency[None, :]
    cosine = jnp.cos(angle)[:, None, :]
    sine = jnp.sin(angle)[:, None, :]
    if inverse:
        sine = -sine
    first_half = pieces[:, :, :half_width]
    second_half = pieces[:, :, half_width:]
    result = jnp.concatenate([first_half * cosine - second_half * sine, second_half * cosine + first_half * sine], axis=2)
    return result.reshape(row_count, -1)

def normalize(values_in):
    center = lax.optimization_barrier(jnp.mean(values_in, axis=-1, keepdims=True))
    centered = values_in - center
    variance = lax.optimization_barrier(jnp.mean(centered * centered, axis=-1, keepdims=True))
    return centered * lax.rsqrt(variance + EPSILON)

def head_scores(query_head, key_head, key_valid):
    scores = jnp.dot(query_head, key_head.T, preferred_element_type=jnp.float32) * (1.0 / math.sqrt(HD))
    return jnp.where(key_valid[None, :], scores, -jnp.inf)

def head_forward(operand, key_valid):
    query_head, key_head, value_head = operand
    scores = head_scores(query_head, key_head, key_valid)
    largest = lax.optimization_barrier(jnp.max(scores, axis=1))
    total = lax.optimization_barrier(jnp.sum(jnp.exp(scores - largest[:, None]), axis=1))
    log_total = largest + jnp.log(total)
    weights = jnp.exp(scores - log_total[:, None])
    output = jnp.dot(weights.astype(jnp.bfloat16), value_head, preferred_element_type=jnp.float32).astype(jnp.bfloat16)
    return (output, log_total)

def head_backward(operand, key_valid):
    query_head, key_head, value_head, out_head, grad_head, log_total = operand
    scores = head_scores(query_head, key_head, key_valid)
    weights = jnp.exp(scores - log_total[:, None])
    weights_low = weights.astype(jnp.bfloat16)
    delta = lax.optimization_barrier(jnp.sum(grad_head.astype(jnp.float32) * out_head.astype(jnp.float32), axis=1))
    value_grad = jnp.dot(weights_low.T, grad_head, preferred_element_type=jnp.float32)
    weight_grad = jnp.dot(grad_head, value_head.T, preferred_element_type=jnp.float32)
    score_grad = (weights * (weight_grad - delta[:, None]) * (1.0 / math.sqrt(HD))).astype(jnp.bfloat16)
    query_grad = jnp.dot(score_grad, key_head, preferred_element_type=jnp.float32)
    key_grad = jnp.dot(score_grad.T, query_head, preferred_element_type=jnp.float32)
    return (query_grad, key_grad, value_grad)

def split_heads(array):
    return array.reshape(array.shape[0], HEADS, HD).transpose(1, 0, 2)

def join_heads(array):
    return array.transpose(1, 0, 2).reshape(array.shape[1], HEADS * HD)

def reference(queries, keys, values, query_frames, frame_counts, clip_of_frame, in_proj, mlp_up, mlp_down, reward_head):
    in_frame = jnp.arange(FTOK, dtype=jnp.int32)
    query_position = (query_frames[:, None] * FTOK + in_frame[None, :]).reshape(-1)
    key_position = jnp.arange(KTOK, dtype=jnp.int32)
    key_valid = (in_frame[None, :] < frame_counts[:, None]).reshape(-1)
    slot_counts = frame_counts[query_frames]
    query_valid = (in_frame[None, :] < slot_counts[:, None]).reshape(-1)
    slot_index = jnp.arange(QFRAMES, dtype=jnp.int32)
    slot_clip = slot_index // QFR_DEV * N_FRAME + clip_of_frame
    row_clip = jnp.repeat(slot_clip, FTOK)
    rotated_query = rotate(queries.astype(jnp.float32), query_position, False).astype(jnp.bfloat16)
    rotated_key = rotate(keys.astype(jnp.float32), key_position, False).astype(jnp.bfloat16)
    query_heads = split_heads(rotated_query)
    key_heads = split_heads(rotated_key)
    value_heads = split_heads(values)
    out_heads, log_totals = lax.map(partial_forward(key_valid), (query_heads, key_heads, value_heads))
    attention_out = join_heads(out_heads)
    clip_inputs = jnp.dot(attention_out, in_proj, preferred_element_type=jnp.float32)

    def score_clips(inputs):
        normed = normalize(inputs).astype(jnp.bfloat16)
        expanded = jax.nn.gelu(jnp.dot(normed, mlp_up, preferred_element_type=jnp.float32)).astype(jnp.bfloat16)
        hidden = jnp.dot(expanded, mlp_down, preferred_element_type=jnp.float32)
        live = query_valid.astype(jnp.float32)
        sums = jax.ops.segment_sum(hidden * live[:, None], row_clip, NCLIPS)
        counts = jax.ops.segment_sum(live, row_clip, NCLIPS)
        pooled = sums / counts[:, None]
        return counts * jnp.dot(normalize(pooled), reward_head, precision=lax.Precision.HIGHEST)
    rewards, pull_back = jax.vjp(score_clips, clip_inputs)
    input_grad, = pull_back(jnp.ones_like(rewards))
    out_grad = jnp.dot(input_grad.astype(jnp.bfloat16), in_proj.T, preferred_element_type=jnp.float32).astype(jnp.bfloat16)
    query_grad, key_grad, value_grad = lax.map(partial_backward(key_valid), (query_heads, key_heads, value_heads, out_heads, split_heads(out_grad), log_totals))
    query_result = rotate(join_heads(query_grad), query_position, True)
    key_result = rotate(join_heads(key_grad), key_position, True)
    return (query_result, key_result, join_heads(value_grad), rewards)

def partial_forward(key_valid):

    def apply_head(operand):
        return head_forward(operand, key_valid)
    return apply_head

def partial_backward(key_valid):

    def apply_head(operand):
        return head_backward(operand, key_valid)
    return apply_head
```

```python
import functools
import math

import jax
import jax.numpy as jnp
import numpy as np
from jax import lax
from jax.experimental import pallas as pl
from jax.experimental.pallas import tpu as pltpu
from jax.sharding import PartitionSpec as P

HD = 128
FTOK = 16
CLIP = 2
EPSILON = 1e-05
NEG = -1e30
LOG2E = math.log2(math.e)
MESH = pl.DeviceIdType.MESH
BF = jnp.bfloat16
F32 = jnp.float32
VCHUNK = 512

NN = (((1,), (0,)), ((), ()))
NT = (((1,), (1,)), ((), ()))


def mm(left, right, dims):
    return lax.dot_general(left, right, dims, preferred_element_type=F32)


def iota(shape, dim):
    return lax.broadcasted_iota(jnp.int32, shape, dim)


def norm_stats(x):
    center = jnp.mean(x, axis=-1, keepdims=True)
    centered = x - center
    inverse = lax.rsqrt(jnp.mean(centered * centered, axis=-1, keepdims=True) + EPSILON)
    return centered * inverse, inverse


def norm_back(grad, hat, inverse):
    return inverse * (
        grad
        - jnp.mean(grad, axis=-1, keepdims=True)
        - hat * jnp.mean(grad * hat, axis=-1, keepdims=True)
    )


def kernel(
    n_ctx,
    n_frame,
    q_ref,
    k_ref,
    v_ref,
    qf_ref,
    fc_ref,
    cf_ref,
    ck_ref,
    sk_ref,
    cq_ref,
    sq_ref,
    ct_ref,
    st_ref,
    ip_ref,
    up_ref,
    down_ref,
    head_ref,
    dq_ref,
    dk_ref,
    dv_ref,
    rew_ref,
    kin,
    vin,
    ip,
    up,
    down,
    qbuf,
    kr,
    krt,
    vt,
    cosk,
    sink,
    osend,
    orecv,
    ssend,
    srecv,
    ot,
    xsend,
    xrecv,
    gbuf,
    gp,
    dobuf,
    sbuf,
    dqsend,
    dqrecv,
    csend,
    crecv,
    fsend,
    frecv,
    local,
):
    me = lax.axis_index("ctx")
    fi = lax.axis_index("frame")
    rows, width = q_ref.shape
    key_rows = k_ref.shape[0]
    heads = width // HD
    slots = qf_ref.shape[1]
    clip_rows = CLIP * FTOK
    vd = ip_ref.shape[1]
    vff = up_ref.shape[1]
    scale = 1.0 / math.sqrt(HD)

    loads = [
        pltpu.make_async_copy(src, dst, local.at[i])
        for i, (src, dst) in enumerate(
            [(k_ref, kin), (v_ref, vin), (ip_ref, ip), (up_ref, up), (down_ref, down)]
        )
    ]
    for load in loads:
        load.start()

    barrier = pltpu.get_barrier_semaphore()
    for d in range(1, n_ctx):
        pl.semaphore_signal(
            barrier, inc=1, device_id={"ctx": lax.rem(me + d, n_ctx)}, device_id_type=MESH
        )
    for d in range(1, n_frame):
        pl.semaphore_signal(
            barrier, inc=1, device_id={"frame": lax.rem(fi + d, n_frame)}, device_id_type=MESH
        )

    def send_ctx(phase, src, dst, offset, index):
        return pltpu.make_async_remote_copy(
            src_ref=src,
            dst_ref=dst,
            send_sem=csend.at[phase, index],
            recv_sem=crecv.at[phase, offset],
            device_id={"ctx": lax.rem(me + offset, n_ctx)},
            device_id_type=MESH,
        )

    def send_frame(phase, src, dst, d):
        return pltpu.make_async_remote_copy(
            src_ref=src,
            dst_ref=dst,
            send_sem=fsend.at[phase, d],
            recv_sem=frecv.at[phase, d],
            device_id={"frame": lax.rem(fi + d, n_frame)},
            device_id_type=MESH,
        )

    def table(cos_a, sin_a, cos_b, sin_b):
        n_a = cos_a.shape[0]
        cos_a, sin_a = cos_a[:, None, :], sin_a[:, None, :]
        cos_b, sin_b = cos_b[None], sin_b[None]
        return (
            (cos_a * cos_b - sin_a * sin_b).reshape(n_a * FTOK, HD),
            (sin_a * cos_b + cos_a * sin_b).reshape(n_a * FTOK, HD),
        )

    cos_t, sin_t = ct_ref[...], st_ref[...]
    cos_q, sin_q = table(cq_ref[...], sq_ref[...], cos_t, sin_t)
    for h in range(heads):
        part = q_ref[:, h * HD : (h + 1) * HD].astype(F32)
        qbuf[0, :, h * HD : (h + 1) * HD] = (
            part * cos_q + pltpu.roll(part, HD // 2, 1) * sin_q
        ).astype(BF)

    pl.semaphore_wait(barrier, n_ctx - 1 + n_frame - 1)
    q_sends = [send_ctx(0, qbuf.at[0], qbuf.at[d], d, d) for d in range(1, n_ctx)]
    for copy in q_sends:
        copy.start()

    cos_k, sin_k = table(ck_ref[...], sk_ref[...], cos_t, sin_t)
    cosk[...] = cos_k
    sink[...] = sin_k
    loads[0].wait()
    loads[1].wait()
    for h in range(heads):
        part = kin[:, h * HD : (h + 1) * HD].astype(F32)
        turned = (part * cosk[...] + pltpu.roll(part, HD // 2, 1) * sink[...]).astype(BF)
        kr[:, h * HD : (h + 1) * HD] = turned
        krt[h * HD : (h + 1) * HD, :] = turned.astype(F32).T.astype(BF)
        vt[h * HD : (h + 1) * HD, :] = vin[:, h * HD : (h + 1) * HD].astype(F32).T.astype(BF)

    live_total = jnp.sum(fc_ref[...].astype(F32), axis=1, keepdims=True)
    key_at = (iota((key_rows, 1), 0) + me * key_rows).astype(F32)
    bias = jnp.where(key_at < live_total, 0.0, NEG)

    def forward(d, out_ref, stat_ref):
        for h in range(heads):
            cols = slice(h * HD, (h + 1) * HD)
            s = mm(kr[:, cols], qbuf[d, :, cols], NT) * (scale * LOG2E) + bias
            top = jnp.max(s, axis=0, keepdims=True)
            p = jnp.exp2(s - top)
            total = jnp.sum(p, axis=0, keepdims=True)
            o = mm(vt[cols, :], p.astype(BF), NN) * (1.0 / total)
            out_ref[cols, :] = o.astype(BF)
            stat_ref[h : h + 1, :] = top + jnp.log2(total)

    ssend[...] = jnp.zeros_like(ssend)
    forward(0, orecv.at[0], srecv.at[0])

    def o_copies(d):
        back = n_ctx - d
        return (
            send_ctx(1, osend.at[d], orecv.at[back], back, d),
            send_ctx(2, ssend.at[d], srecv.at[back], back, d),
        )

    @pl.loop(1, n_ctx)
    def _(d):
        send_ctx(0, qbuf.at[0], qbuf.at[d], d, d).wait_recv()
        forward(d, osend.at[d], ssend.at[d])
        for copy in o_copies(d):
            copy.start()

    clip_row = cf_ref[...].astype(F32)
    eye = iota((slots, slots), 0) == iota((slots, slots), 1)
    clip_col = jnp.sum(jnp.where(eye, clip_row, 0.0), axis=1, keepdims=True)
    frame_col = jnp.sum(jnp.where(eye, qf_ref[...].astype(F32), 0.0), axis=1, keepdims=True)
    earlier = jnp.logical_and(
        clip_col == clip_row, iota((slots, slots), 1) < iota((slots, slots), 0)
    )
    dest_col = clip_col * CLIP + jnp.sum(jnp.where(earlier, 1.0, 0.0), axis=1, keepdims=True)
    dest_row = jnp.sum(jnp.where(eye, dest_col, 0.0), axis=0, keepdims=True)
    wide_row = (
        jnp.sum(
            jnp.where(iota((slots, rows), 0) == lax.div(iota((slots, rows), 1), FTOK), dest_col, 0.0),
            axis=0,
            keepdims=True,
        )
        * FTOK
        + lax.rem(iota((1, rows), 1), FTOK).astype(F32)
    )
    wide_col = (
        jnp.sum(
            jnp.where(lax.div(iota((rows, slots), 0), FTOK) == iota((rows, slots), 1), dest_row, 0.0),
            axis=1,
            keepdims=True,
        )
        * FTOK
        + lax.rem(iota((rows, 1), 0), FTOK).astype(F32)
    )
    to_group = jnp.where(iota((rows, rows), 0).astype(F32) == wide_row, 1.0, 0.0).astype(BF)
    from_group = jnp.where(iota((rows, rows), 1).astype(F32) == wide_col, 1.0, 0.0).astype(BF)
    count_col = jnp.clip(live_total - frame_col * FTOK, 0.0, float(FTOK))
    live = jnp.zeros((clip_rows, 1), F32)
    count = jnp.zeros((1, 1), F32)
    for j in range(CLIP):
        mine = (fi * CLIP + j).astype(F32)
        tokens = jnp.sum(jnp.where(dest_col == mine, count_col, 0.0), axis=0, keepdims=True)
        at = (iota((clip_rows, 1), 0) - j * FTOK).astype(F32)
        live = live + jnp.where(jnp.logical_and(at >= 0.0, at < tokens), 1.0, 0.0)
        count = count + tokens

    loads[2].wait()
    for d in range(1, n_ctx):
        send_ctx(1, osend.at[d], orecv.at[d], d, d).wait_recv()
        send_ctx(2, ssend.at[d], srecv.at[d], d, d).wait_recv()
    sbuf[0] = jnp.zeros_like(sbuf[0])
    for h in range(heads):
        cols = slice(h * HD, (h + 1) * HD)
        logs = [srecv[c, h : h + 1, :] for c in range(n_ctx)]
        top = functools.reduce(jnp.maximum, logs)
        shares = [jnp.exp2(x - top) for x in logs]
        total = functools.reduce(jnp.add, shares)
        inverse = 1.0 / total
        acc = jnp.zeros((HD, rows), F32)
        for c in range(n_ctx):
            acc = acc + orecv[c, cols, :].astype(F32) * (shares[c] * inverse)
        ot[cols, :] = acc.astype(BF)
        sbuf[0, h : h + 1, :] = top + jnp.log2(total)

    grouped = mm(to_group, ot[...], NT).astype(BF)
    shares = mm(grouped, ip[...], NN).astype(BF)
    for f in range(n_frame):
        xsend[f] = shares[f * clip_rows : (f + 1) * clip_rows, :]
    x_sends = [
        send_frame(0, xsend.at[lax.rem(fi + d, n_frame)], xrecv.at[d], d) for d in range(1, n_frame)
    ]
    for copy in x_sends:
        copy.start()
    x = xsend[fi].astype(F32)
    for d in range(1, n_frame):
        x_sends[d - 1].wait_recv()
        x = x + xrecv[d].astype(F32)

    hat, inverse = norm_stats(x)
    y = hat.astype(BF)
    loads[3].wait()
    loads[4].wait()
    c0 = math.sqrt(2.0 / math.pi)
    c1 = 0.044715

    def mlp_step(j, hidden):
        cols = pl.ds(pl.multiple_of(j * VCHUNK, VCHUNK), VCHUNK)
        u = mm(y, up[:, cols], NN)
        t = jnp.tanh(c0 * (u + c1 * u * u * u))
        e = (0.5 * u * (1.0 + t)).astype(BF)
        gp[:, cols] = 0.5 * (1.0 + t) + 0.5 * u * (1.0 - t * t) * (c0 * (1.0 + 3.0 * c1 * u * u))
        return hidden + mm(e, down[cols, :], NN)

    hidden = lax.fori_loop(0, vff // VCHUNK, mlp_step, jnp.zeros((clip_rows, vd), F32))
    pooled = jnp.sum(hidden * live, axis=0, keepdims=True) / count
    pooled_hat, pooled_inverse = norm_stats(pooled)
    weight = head_ref[...]
    rew_ref[...] = count * jnp.sum(pooled_hat * weight, axis=1, keepdims=True)
    d_hidden = norm_back(weight, pooled_hat, pooled_inverse)
    high = d_hidden.astype(BF).astype(F32)
    pick = iota((16, vd), 0)
    pair = jnp.where(
        pick == 0, high, jnp.where(pick == 1, d_hidden - high, 0.0)
    ).astype(BF)

    def back_step(j, d_y):
        cols = pl.ds(pl.multiple_of(j * VCHUNK, VCHUNK), VCHUNK)
        both = mm(pair, down[cols, :], NT)
        d_e = both[0:1, :] + both[1:2, :]
        d_u = (live * d_e * gp[:, cols]).astype(BF)
        return d_y + mm(d_u, up[:, cols], NT)

    d_y = lax.fori_loop(0, vff // VCHUNK, back_step, jnp.zeros((clip_rows, vd), F32))
    gbuf[fi] = norm_back(d_y, hat, inverse).astype(BF)
    g_sends = [send_frame(1, gbuf.at[fi], gbuf.at[fi], d) for d in range(1, n_frame)]
    for copy in g_sends:
        copy.start()
    for d in range(1, n_frame):
        source = lax.rem(fi + n_frame - d, n_frame)
        send_frame(1, gbuf.at[source], gbuf.at[source], d).wait_recv()
    g = gbuf[...].reshape(rows, vd)
    grouped_grad = mm(g, ip[...], NT).astype(BF)
    out_grad = mm(from_group, grouped_grad, NN)
    dobuf[0] = out_grad.astype(BF)
    for h in range(heads):
        cols = slice(h * HD, (h + 1) * HD)
        turned = out_grad[:, cols].T
        sbuf[0, heads + h : heads + h + 1, :] = jnp.sum(
            turned * ot[cols, :].astype(F32), axis=0, keepdims=True
        )
    do_sends = []
    for d in range(1, n_ctx):
        do_sends.append(send_ctx(3, dobuf.at[0], dobuf.at[d], d, d))
        do_sends.append(send_ctx(4, sbuf.at[0], sbuf.at[d], d, d))
    for copy in do_sends:
        copy.start()

    def backward(d, out_ref, first):
        for h in range(heads):
            cols = slice(h * HD, (h + 1) * HD)
            q_head = qbuf[d, :, cols]
            do_head = dobuf[d, :, cols]
            s = mm(kr[:, cols], q_head, NT) * (scale * LOG2E) + bias
            p = jnp.exp2(s - sbuf[d, h : h + 1, :])
            dp = mm(vin[:, cols], do_head, NT)
            ds = (p * (dp - sbuf[d, heads + h : heads + h + 1, :]) * scale).astype(BF)
            dv = mm(p.astype(BF), do_head, NN)
            dk = mm(ds, q_head, NN)
            if first:
                dv_ref[:, cols] = dv
                dk_ref[:, cols] = dk
            else:
                dv_ref[:, cols] = dv_ref[:, cols] + dv
                dk_ref[:, cols] = dk_ref[:, cols] + dk
            out_ref[cols, :] = mm(krt[cols, :], ds, NN).astype(BF)

    backward(0, dqrecv.at[0], True)

    def dq_copy(d):
        back = n_ctx - d
        return send_ctx(5, dqsend.at[d], dqrecv.at[back], back, d)

    @pl.loop(1, n_ctx)
    def _(d):
        send_ctx(3, dobuf.at[0], dobuf.at[d], d, d).wait_recv()
        send_ctx(4, sbuf.at[0], sbuf.at[d], d, d).wait_recv()
        backward(d, dqsend.at[d], False)
        dq_copy(d).start()

    for h in range(heads):
        cols = slice(h * HD, (h + 1) * HD)
        part = dk_ref[:, cols]
        dk_ref[:, cols] = part * cosk[...] - pltpu.roll(part, HD // 2, 1) * sink[...]

    for d in range(1, n_ctx):
        send_ctx(5, dqsend.at[d], dqrecv.at[d], d, d).wait_recv()
    cos_q, sin_q = table(cq_ref[...], sq_ref[...], ct_ref[...], st_ref[...])
    for h in range(heads):
        cols = slice(h * HD, (h + 1) * HD)
        acc = dqrecv[0, cols, :].astype(F32)
        for c in range(1, n_ctx):
            acc = acc + dqrecv[c, cols, :].astype(F32)
        part = acc.T
        dq_ref[:, cols] = part * cos_q - pltpu.roll(part, HD // 2, 1) * sin_q

    for copy in q_sends + x_sends + g_sends + do_sends:
        copy.wait_send()
    for d in range(1, n_ctx):
        for copy in o_copies(d):
            copy.wait_send()
        dq_copy(d).wait_send()


def shards(
    n_ctx,
    n_frame,
    queries,
    keys,
    values,
    query_frames,
    frame_counts,
    clip_of_frame,
    in_proj,
    mlp_up,
    mlp_down,
    reward_head,
):
    rows, width = queries.shape
    key_rows = keys.shape[0]
    key_frames = key_rows // FTOK
    vd, vff = mlp_up.shape
    half = HD // 2
    clip_rows = CLIP * FTOK
    lane = np.arange(HD) % half
    frequency = jnp.asarray(
        np.exp(-math.log(10000.0) * lane / half).astype(np.float32)
    )
    sign = jnp.asarray(np.where(np.arange(HD) < half, -1.0, 1.0).astype(np.float32))

    def trig(position):
        angle = position.astype(F32)[:, None] * frequency[None, :]
        return jnp.cos(angle), jnp.sin(angle) * sign[None, :]

    first_frame = lax.axis_index("ctx") * key_frames
    cos_k, sin_k = trig((first_frame + jnp.arange(key_frames, dtype=jnp.int32)) * FTOK)
    cos_q, sin_q = trig(query_frames * FTOK)
    cos_t, sin_t = trig(jnp.arange(FTOK, dtype=jnp.int32))

    vmem = pl.BlockSpec(memory_space=pltpu.VMEM)
    hbm = pl.BlockSpec(memory_space=pl.ANY)
    call = pl.pallas_call(
        functools.partial(kernel, n_ctx, n_frame),
        out_shape=(
            jax.ShapeDtypeStruct((rows, width), F32),
            jax.ShapeDtypeStruct((key_rows, width), F32),
            jax.ShapeDtypeStruct((key_rows, width), F32),
            jax.ShapeDtypeStruct((1, 1), F32),
        ),
        in_specs=[vmem, hbm, hbm] + [vmem] * 9 + [hbm] * 3 + [vmem],
        out_specs=(vmem, vmem, vmem, vmem),
        scratch_shapes=[
            pltpu.VMEM((key_rows, width), BF),
            pltpu.VMEM((key_rows, width), BF),
            pltpu.VMEM((width, vd), BF),
            pltpu.VMEM((vd, vff), BF),
            pltpu.VMEM((vff, vd), BF),
            pltpu.VMEM((n_ctx, rows, width), BF),
            pltpu.VMEM((key_rows, width), BF),
            pltpu.VMEM((width, key_rows), BF),
            pltpu.VMEM((width, key_rows), BF),
            pltpu.VMEM((key_rows, HD), F32),
            pltpu.VMEM((key_rows, HD), F32),
            pltpu.VMEM((n_ctx, width, rows), BF),
            pltpu.VMEM((n_ctx, width, rows), BF),
            pltpu.VMEM((n_ctx, 8, rows), F32),
            pltpu.VMEM((n_ctx, 8, rows), F32),
            pltpu.VMEM((width, rows), BF),
            pltpu.VMEM((n_frame, clip_rows, vd), BF),
            pltpu.VMEM((n_frame, clip_rows, vd), BF),
            pltpu.VMEM((n_frame, clip_rows, vd), BF),
            pltpu.VMEM((clip_rows, vff), F32),
            pltpu.VMEM((n_ctx, rows, width), BF),
            pltpu.VMEM((n_ctx, 8, rows), F32),
            pltpu.VMEM((n_ctx, width, rows), BF),
            pltpu.VMEM((n_ctx, width, rows), BF),
            pltpu.SemaphoreType.DMA((6, n_ctx)),
            pltpu.SemaphoreType.DMA((6, n_ctx)),
            pltpu.SemaphoreType.DMA((2, n_frame)),
            pltpu.SemaphoreType.DMA((2, n_frame)),
            pltpu.SemaphoreType.DMA((5,)),
        ],
        compiler_params=pltpu.CompilerParams(
            collective_id=0, has_side_effects=True, vmem_limit_bytes=60 * 1024 * 1024
        ),
    )
    query_grad, key_grad, value_grad, reward = call(
        queries,
        keys,
        values,
        query_frames.reshape(1, -1),
        frame_counts.reshape(1, -1),
        clip_of_frame.reshape(1, -1),
        cos_k,
        sin_k,
        cos_q,
        sin_q,
        cos_t,
        sin_t,
        in_proj,
        mlp_up,
        mlp_down,
        reward_head.reshape(1, -1),
    )
    return query_grad, key_grad, value_grad, reward.reshape(1)


def solution(mesh):
    return jax.shard_map(
        functools.partial(shards, mesh.shape["ctx"], mesh.shape["frame"]),
        mesh=mesh,
        in_specs=(
            P("ctx", "frame"),
            P("ctx", "frame"),
            P("ctx", "frame"),
            P("ctx"),
            P(),
            P("ctx"),
            P("frame", None),
            P(),
            P(),
            P(),
        ),
        out_specs=(P("ctx", "frame"), P("ctx", "frame"), P("ctx", "frame"), P(("ctx", "frame"))),
        check_vma=False,
    )
```

```python
import functools
import math

import jax
import jax.numpy as jnp
import numpy as np
from jax import lax
from jax.experimental import pallas as pl
from jax.experimental.pallas import tpu as pltpu
from jax.sharding import PartitionSpec as P

HD = 128
FTOK = 16
CLIP = 2
EPSILON = 1e-05
NEG = -1e30
LOG2E = math.log2(math.e)
MESH = pl.DeviceIdType.MESH
BF = jnp.bfloat16
F32 = jnp.float32
VCHUNK = 512
PIECES = 4

NN = (((1,), (0,)), ((), ()))
NT = (((1,), (1,)), ((), ()))


def mm(left, right, dims):
    return lax.dot_general(left, right, dims, preferred_element_type=F32)


def iota(shape, dim):
    return lax.broadcasted_iota(jnp.int32, shape, dim)


def norm_stats(x):
    center = jnp.mean(x, axis=-1, keepdims=True)
    centered = x - center
    inverse = lax.rsqrt(jnp.mean(centered * centered, axis=-1, keepdims=True) + EPSILON)
    return centered * inverse, inverse


def norm_back(grad, hat, inverse):
    return inverse * (
        grad
        - jnp.mean(grad, axis=-1, keepdims=True)
        - hat * jnp.mean(grad * hat, axis=-1, keepdims=True)
    )


def kernel(
    n_ctx,
    n_frame,
    q_ref,
    k_ref,
    v_ref,
    qf_ref,
    fc_ref,
    cf_ref,
    cos_ref,
    sin_ref,
    ip_ref,
    up_ref,
    down_ref,
    head_ref,
    dq_ref,
    dk_ref,
    dv_ref,
    rew_ref,
    kin,
    vin,
    ip,
    up,
    down,
    qbuf,
    krt,
    vt,
    cosk,
    sink,
    cosq,
    sinq,
    osend,
    orecv,
    ssend,
    srecv,
    ot,
    xsend,
    xpair,
    xsum,
    xrecv,
    gbuf,
    gp,
    dobuf,
    lbuf,
    sbuf,
    stash,
    dkacc,
    dvacc,
    dqrecv,
    csend,
    crecv,
    fsend,
    frecv,
    local,
):
    me = lax.axis_index("ctx")
    fi = lax.axis_index("frame")
    rows, width = q_ref.shape
    key_rows = k_ref.shape[0]
    heads = width // HD
    slots = qf_ref.shape[1]
    clip_rows = CLIP * FTOK
    vd = ip_ref.shape[1]
    vff = up_ref.shape[1]
    key_frames = key_rows // FTOK
    scale = 1.0 / math.sqrt(HD)
    n_deep = n_frame // 2
    core, deep = lax.rem(fi, 2), lax.div(fi, 2)
    sibling = fi + 1 - 2 * core

    def deep_peer(d):
        return lax.rem(deep + d, n_deep) * 2 + core

    loads = [
        pltpu.make_async_copy(src, dst, local.at[i])
        for i, (src, dst) in enumerate(
            [(k_ref, kin), (v_ref, vin), (ip_ref, ip), (up_ref, up), (down_ref, down)]
        )
    ]
    for load in loads:
        load.start()

    barrier = pltpu.get_barrier_semaphore()
    for d in range(1, n_ctx):
        pl.semaphore_signal(
            barrier, inc=1, device_id={"ctx": lax.rem(me + d, n_ctx)}, device_id_type=MESH
        )
    for peer in [sibling] + [deep_peer(d) for d in range(1, n_deep)]:
        pl.semaphore_signal(barrier, inc=1, device_id={"frame": peer}, device_id_type=MESH)

    def send_ctx(phase, src, dst, offset, index):
        return pltpu.make_async_remote_copy(
            src_ref=src,
            dst_ref=dst,
            send_sem=csend.at[phase, index],
            recv_sem=crecv.at[phase, offset],
            device_id={"ctx": lax.rem(me + offset, n_ctx)},
            device_id_type=MESH,
        )

    def send_frame(phase, src, dst, peer, d):
        return pltpu.make_async_remote_copy(
            src_ref=src,
            dst_ref=dst,
            send_sem=fsend.at[phase, d],
            recv_sem=frecv.at[phase, d],
            device_id={"frame": peer},
            device_id_type=MESH,
        )

    def table(cos_a, sin_a, cos_b, sin_b):
        n_a = cos_a.shape[0]
        cos_a, sin_a = cos_a[:, None, :], sin_a[:, None, :]
        cos_b, sin_b = cos_b[None], sin_b[None]
        return (
            (cos_a * cos_b - sin_a * sin_b).reshape(n_a * FTOK, HD),
            (sin_a * cos_b + cos_a * sin_b).reshape(n_a * FTOK, HD),
        )

    all_frames = cos_ref.shape[0] - FTOK
    cos_t, sin_t = cos_ref[all_frames:, :], sin_ref[all_frames:, :]
    eye = iota((slots, slots), 0) == iota((slots, slots), 1)
    frame_col = jnp.sum(jnp.where(eye, qf_ref[...].astype(F32), 0.0), axis=1, keepdims=True)
    choose = jnp.where(iota((slots, all_frames), 1).astype(F32) == frame_col, 1.0, 0.0)

    def chosen(ref):
        return lax.dot_general(
            choose,
            ref[:all_frames, :],
            NN,
            precision=lax.Precision.HIGHEST,
            preferred_element_type=F32,
        )

    cos_q, sin_q = table(chosen(cos_ref), chosen(sin_ref), cos_t, sin_t)
    cosq[...] = cos_q
    sinq[...] = sin_q
    for h in range(heads):
        part = q_ref[:, h * HD : (h + 1) * HD].astype(F32)
        qbuf[0, :, h * HD : (h + 1) * HD] = (
            part * cos_q + pltpu.roll(part, HD // 2, 1) * sin_q
        ).astype(BF)

    pl.semaphore_wait(barrier, n_ctx - 1 + n_deep)
    q_sends = [send_ctx(0, qbuf.at[0], qbuf.at[d], d, d) for d in range(1, n_ctx)]
    for copy in q_sends:
        copy.start()

    own_frames = pl.ds(pl.multiple_of(me * key_frames, 8), key_frames)
    cos_k, sin_k = table(cos_ref[own_frames, :], sin_ref[own_frames, :], cos_t, sin_t)
    cosk[...] = cos_k
    sink[...] = sin_k
    loads[0].wait()
    loads[1].wait()
    for h in range(heads):
        part = kin[:, h * HD : (h + 1) * HD].astype(F32)
        turned = (part * cosk[...] + pltpu.roll(part, HD // 2, 1) * sink[...]).astype(BF)
        kin[:, h * HD : (h + 1) * HD] = turned
        krt[h * HD : (h + 1) * HD, :] = turned.astype(F32).T.astype(BF)
        vt[h * HD : (h + 1) * HD, :] = vin[:, h * HD : (h + 1) * HD].astype(F32).T.astype(BF)

    live_total = jnp.sum(fc_ref[...].astype(F32), axis=1, keepdims=True)
    key_at = (iota((key_rows, 1), 0) + me * key_rows).astype(F32)
    bias = jnp.where(key_at < live_total, 0.0, NEG)

    def forward(d, out_ref, stat_ref):
        for h in range(heads):
            cols = slice(h * HD, (h + 1) * HD)
            s = mm(kin[:, cols], qbuf[d, :, cols], NT) * (scale * LOG2E) + bias
            top = jnp.max(s, axis=0, keepdims=True)
            p = jnp.exp2(s - top)
            total = jnp.sum(p, axis=0, keepdims=True)
            o = mm(vt[cols, :], p.astype(BF), NN) * (1.0 / total)
            out_ref[cols, :] = o.astype(BF)
            stat_ref[h : h + 1, :] = top + jnp.log2(total)

    ssend[...] = jnp.zeros_like(ssend)
    forward(0, orecv.at[0], srecv.at[0])

    def o_copies(d):
        back = n_ctx - d
        return (
            send_ctx(1, osend.at[d], orecv.at[back], back, d),
            send_ctx(2, ssend.at[d], srecv.at[back], back, d),
        )

    @pl.loop(1, n_ctx)
    def _(d):
        send_ctx(0, qbuf.at[0], qbuf.at[d], d, d).wait_recv()
        forward(d, osend.at[d], ssend.at[d])
        for copy in o_copies(d):
            copy.start()

    clip_row = cf_ref[...].astype(F32)
    clip_col = jnp.sum(jnp.where(eye, clip_row, 0.0), axis=1, keepdims=True)
    earlier = jnp.logical_and(
        clip_col == clip_row, iota((slots, slots), 1) < iota((slots, slots), 0)
    )
    dest_col = clip_col * CLIP + jnp.sum(jnp.where(earlier, 1.0, 0.0), axis=1, keepdims=True)
    dest_row = jnp.sum(jnp.where(eye, dest_col, 0.0), axis=0, keepdims=True)
    wide_row = (
        jnp.sum(
            jnp.where(iota((slots, rows), 0) == lax.div(iota((slots, rows), 1), FTOK), dest_col, 0.0),
            axis=0,
            keepdims=True,
        )
        * FTOK
        + lax.rem(iota((1, rows), 1), FTOK).astype(F32)
    )
    wide_col = (
        jnp.sum(
            jnp.where(lax.div(iota((rows, slots), 0), FTOK) == iota((rows, slots), 1), dest_row, 0.0),
            axis=1,
            keepdims=True,
        )
        * FTOK
        + lax.rem(iota((rows, 1), 0), FTOK).astype(F32)
    )
    to_group = jnp.where(iota((rows, rows), 0).astype(F32) == wide_row, 1.0, 0.0).astype(BF)
    from_group = jnp.where(iota((rows, rows), 1).astype(F32) == wide_col, 1.0, 0.0).astype(BF)
    count_col = jnp.clip(live_total - frame_col * FTOK, 0.0, float(FTOK))
    live = jnp.zeros((clip_rows, 1), F32)
    count = jnp.zeros((1, 1), F32)
    for j in range(CLIP):
        mine = (fi * CLIP + j).astype(F32)
        tokens = jnp.sum(jnp.where(dest_col == mine, count_col, 0.0), axis=0, keepdims=True)
        at = (iota((clip_rows, 1), 0) - j * FTOK).astype(F32)
        live = live + jnp.where(jnp.logical_and(at >= 0.0, at < tokens), 1.0, 0.0)
        count = count + tokens

    loads[2].wait()
    for d in range(1, n_ctx):
        send_ctx(1, osend.at[d], orecv.at[d], d, d).wait_recv()
        send_ctx(2, ssend.at[d], srecv.at[d], d, d).wait_recv()
    lbuf[0] = jnp.zeros_like(lbuf[0])
    sbuf[0] = jnp.zeros_like(sbuf[0])
    for h in range(heads):
        cols = slice(h * HD, (h + 1) * HD)
        logs = [srecv[c, h : h + 1, :] for c in range(n_ctx)]
        top = functools.reduce(jnp.maximum, logs)
        shares = [jnp.exp2(x - top) for x in logs]
        total = functools.reduce(jnp.add, shares)
        inverse = 1.0 / total
        acc = jnp.zeros((HD, rows), F32)
        for c in range(n_ctx):
            acc = acc + orecv[c, cols, :].astype(F32) * (shares[c] * inverse)
        ot[cols, :] = acc.astype(BF)
        lbuf[0, h : h + 1, :] = top + jnp.log2(total)
    l_sends = [send_ctx(6, lbuf.at[0], lbuf.at[d], d, d) for d in range(1, n_ctx)]
    for copy in l_sends:
        copy.start()

    grouped = mm(to_group, ot[...], NT).astype(BF)
    shares = mm(grouped, ip[...], NN).astype(BF)
    for f in range(n_frame):
        xsend[f % 2, f // 2] = shares[f * clip_rows : (f + 1) * clip_rows, :]
    pair_send = send_frame(3, xsend.at[1 - core], xpair, sibling, 0)
    pair_send.start()
    pair_send.wait_recv()
    xsum[...] = (xsend[core].astype(F32) + xpair[...].astype(F32)).astype(BF)
    x_sends = [
        send_frame(0, xsum.at[lax.rem(deep + d, n_deep)], xrecv.at[d], deep_peer(d), d)
        for d in range(1, n_deep)
    ]
    for copy in x_sends:
        copy.start()

    def keep_weights(d):
        for h in range(heads):
            cols = slice(h * HD, (h + 1) * HD)
            s = mm(kin[:, cols], qbuf[d, :, cols], NT) * (scale * LOG2E) + bias
            stash[d * heads + h] = jnp.exp2(s - lbuf[d, h : h + 1, :]).astype(BF)

    keep_weights(0)

    @pl.loop(1, n_ctx)
    def _(d):
        send_ctx(6, lbuf.at[0], lbuf.at[d], d, d).wait_recv()
        keep_weights(d)

    x = xsend[core, deep].astype(F32) + xpair[deep].astype(F32)
    for d in range(1, n_deep):
        x_sends[d - 1].wait_recv()
        x = x + xrecv[d].astype(F32)

    hat, inverse = norm_stats(x)
    y = hat.astype(BF)
    loads[3].wait()
    loads[4].wait()
    c0 = math.sqrt(2.0 / math.pi)
    c1 = 0.044715

    def mlp_step(j, hidden):
        cols = pl.ds(pl.multiple_of(j * VCHUNK, VCHUNK), VCHUNK)
        u = mm(y, up[:, cols], NN)
        t = jnp.tanh(c0 * (u + c1 * u * u * u))
        e = (0.5 * u * (1.0 + t)).astype(BF)
        gp[:, cols] = 0.5 * (1.0 + t) + 0.5 * u * (1.0 - t * t) * (c0 * (1.0 + 3.0 * c1 * u * u))
        return hidden + mm(e, down[cols, :], NN)

    hidden = lax.fori_loop(0, vff // VCHUNK, mlp_step, jnp.zeros((clip_rows, vd), F32))
    pooled = jnp.sum(hidden * live, axis=0, keepdims=True) / count
    pooled_hat, pooled_inverse = norm_stats(pooled)
    weight = head_ref[...]
    rew_ref[...] = count * jnp.sum(pooled_hat * weight, axis=1, keepdims=True)
    d_hidden = norm_back(weight, pooled_hat, pooled_inverse)
    high = d_hidden.astype(BF).astype(F32)
    pick = iota((16, vd), 0)
    pair = jnp.where(
        pick == 0, high, jnp.where(pick == 1, d_hidden - high, 0.0)
    ).astype(BF)

    def back_step(j, d_y):
        cols = pl.ds(pl.multiple_of(j * VCHUNK, VCHUNK), VCHUNK)
        both = mm(pair, down[cols, :], NT)
        d_e = both[0:1, :] + both[1:2, :]
        d_u = (live * d_e * gp[:, cols]).astype(BF)
        return d_y + mm(d_u, up[:, cols], NT)

    d_y = lax.fori_loop(0, vff // VCHUNK, back_step, jnp.zeros((clip_rows, vd), F32))
    gbuf[fi] = norm_back(d_y, hat, inverse).astype(BF)
    g_sends = [send_frame(1, gbuf.at[fi], gbuf.at[fi], deep_peer(d), d) for d in range(1, n_deep)]
    g_sends.append(send_frame(2, gbuf.at[fi], gbuf.at[fi], sibling, 0))
    for copy in g_sends:
        copy.start()
    for d in range(1, n_deep):
        source = deep_peer(n_deep - d)
        send_frame(1, gbuf.at[source], gbuf.at[source], deep_peer(d), d).wait_recv()
        forward_copy = send_frame(2, gbuf.at[source], gbuf.at[source], sibling, d)
        forward_copy.start()
        g_sends.append(forward_copy)
    for d in range(n_deep):
        source = lax.rem(deep + n_deep - d, n_deep) * 2 + 1 - core
        send_frame(2, gbuf.at[source], gbuf.at[source], sibling, d).wait_recv()
    g = gbuf[...].reshape(rows, vd)
    grouped_grad = mm(g, ip[...], NT).astype(BF)
    out_grad = mm(from_group, grouped_grad, NN)
    dobuf[0] = out_grad.astype(BF)
    for h in range(heads):
        cols = slice(h * HD, (h + 1) * HD)
        turned = out_grad[:, cols].T
        sbuf[0, h : h + 1, :] = jnp.sum(
            turned * ot[cols, :].astype(F32), axis=0, keepdims=True
        )
    do_sends = []
    for d in range(1, n_ctx):
        do_sends.append(send_ctx(3, dobuf.at[0], dobuf.at[d], d, d))
        do_sends.append(send_ctx(4, sbuf.at[0], sbuf.at[d], d, d))
    for copy in do_sends:
        copy.start()

    def backward(d, out_ref, first):
        for h in range(heads):
            cols = slice(h * HD, (h + 1) * HD)
            q_head = qbuf[d, :, cols]
            do_head = dobuf[d, :, cols]
            p = stash[d * heads + h]
            dp = mm(vin[:, cols], do_head, NT)
            ds = (p.astype(F32) * (dp - sbuf[d, h : h + 1, :]) * scale).astype(BF)
            dv = mm(p, do_head, NN)
            dk = mm(ds, q_head, NN)
            if first:
                dvacc[:, cols] = dv
                dkacc[:, cols] = dk
            else:
                dvacc[:, cols] = dvacc[:, cols] + dv
                dkacc[:, cols] = dkacc[:, cols] + dk
            out_ref[cols, :] = mm(krt[cols, :], ds, NN).astype(BF)

    for d in range(1, n_ctx):
        for copy in o_copies(d):
            copy.wait_send()
    backward(0, dqrecv.at[0], True)

    def dq_copy(d):
        back = n_ctx - d
        return send_ctx(5, osend.at[d], dqrecv.at[back], back, d)

    @pl.loop(1, n_ctx)
    def _(d):
        send_ctx(3, dobuf.at[0], dobuf.at[d], d, d).wait_recv()
        send_ctx(4, sbuf.at[0], sbuf.at[d], d, d).wait_recv()
        backward(d, osend.at[d], False)
        dq_copy(d).start()

    dv_store = pltpu.make_async_copy(dvacc, dv_ref, local.at[5])
    dv_store.start()
    for h in range(heads):
        cols = slice(h * HD, (h + 1) * HD)
        part = dkacc[:, cols]
        dkacc[:, cols] = part * cosk[...] - pltpu.roll(part, HD // 2, 1) * sink[...]

    dk_store = pltpu.make_async_copy(dkacc, dk_ref, local.at[6])
    dk_store.start()
    for d in range(1, n_ctx):
        send_ctx(5, osend.at[d], dqrecv.at[d], d, d).wait_recv()
    for h in range(heads):
        cols = slice(h * HD, (h + 1) * HD)
        acc = dqrecv[0, cols, :].astype(F32)
        for c in range(1, n_ctx):
            acc = acc + dqrecv[c, cols, :].astype(F32)
        part = acc.T
        dq_ref[:, cols] = part * cosq[...] - pltpu.roll(part, HD // 2, 1) * sinq[...]

    for copy in q_sends + l_sends + [pair_send] + x_sends + g_sends + do_sends:
        copy.wait_send()
    dv_store.wait()
    dk_store.wait()
    for d in range(1, n_ctx):
        dq_copy(d).wait_send()


def deliver_kernel(*refs):
    count = (len(refs) - 1) // 2
    sems = refs[-1]
    copies = []
    for i in range(count):
        for j in range(PIECES):
            step = refs[i].shape[0] // PIECES
            part = pl.ds(j * step, step)
            copies.append(
                pltpu.make_async_copy(
                    refs[i].at[part], refs[count + i].at[part], sems.at[i * PIECES + j]
                )
            )
    for copy in copies:
        copy.start()
    for copy in copies:
        copy.wait()


def deliver(*arrays):
    hbm = pl.BlockSpec(memory_space=pl.ANY)
    return pl.pallas_call(
        deliver_kernel,
        out_shape=tuple(jax.ShapeDtypeStruct(a.shape, a.dtype) for a in arrays),
        in_specs=[hbm] * len(arrays),
        out_specs=(hbm,) * len(arrays),
        scratch_shapes=[pltpu.SemaphoreType.DMA((len(arrays) * PIECES,))],
        compiler_params=pltpu.CompilerParams(vmem_limit_bytes=60 * 1024 * 1024),
    )(*arrays)


def shards(
    n_ctx,
    n_frame,
    queries,
    keys,
    values,
    query_frames,
    frame_counts,
    clip_of_frame,
    in_proj,
    mlp_up,
    mlp_down,
    reward_head,
):
    rows, width = queries.shape
    key_rows = keys.shape[0]
    vd, vff = mlp_up.shape
    half = HD // 2
    heads = width // HD
    n_deep = n_frame // 2
    clip_rows = CLIP * FTOK
    lane = np.arange(HD) % half
    frequency = np.exp(-math.log(10000.0) * lane / half).astype(np.float32)
    sign = np.where(np.arange(HD) < half, -1.0, 1.0)

    position = np.concatenate([np.arange(frame_counts.shape[0]) * FTOK, np.arange(FTOK)])
    angle = (position.astype(np.float32)[:, None] * frequency[None, :]).astype(np.float64)
    cosines = jnp.asarray(np.cos(angle).astype(np.float32))
    sines = jnp.asarray((np.sin(angle) * sign[None, :]).astype(np.float32))

    vmem = pl.BlockSpec(memory_space=pltpu.VMEM)
    hbm = pl.BlockSpec(memory_space=pl.ANY)
    call = pl.pallas_call(
        functools.partial(kernel, n_ctx, n_frame),
        out_shape=(
            jax.ShapeDtypeStruct((rows, width), F32),
            jax.ShapeDtypeStruct((key_rows, width), F32),
            jax.ShapeDtypeStruct((key_rows, width), F32),
            jax.ShapeDtypeStruct((1, 1), F32),
        ),
        in_specs=[vmem, hbm, hbm] + [vmem] * 5 + [hbm] * 3 + [vmem],
        out_specs=(vmem, hbm, hbm, vmem),
        scratch_shapes=[
            pltpu.VMEM((key_rows, width), BF),
            pltpu.VMEM((key_rows, width), BF),
            pltpu.VMEM((width, vd), BF),
            pltpu.VMEM((vd, vff), BF),
            pltpu.VMEM((vff, vd), BF),
            pltpu.VMEM((n_ctx, rows, width), BF),
            pltpu.VMEM((width, key_rows), BF),
            pltpu.VMEM((width, key_rows), BF),
            pltpu.VMEM((key_rows, HD), F32),
            pltpu.VMEM((key_rows, HD), F32),
            pltpu.VMEM((rows, HD), F32),
            pltpu.VMEM((rows, HD), F32),
            pltpu.VMEM((n_ctx, width, rows), BF),
            pltpu.VMEM((n_ctx, width, rows), BF),
            pltpu.VMEM((n_ctx, 8, rows), F32),
            pltpu.VMEM((n_ctx, 8, rows), F32),
            pltpu.VMEM((width, rows), BF),
            pltpu.VMEM((2, n_deep, clip_rows, vd), BF),
            pltpu.VMEM((n_deep, clip_rows, vd), BF),
            pltpu.VMEM((n_deep, clip_rows, vd), BF),
            pltpu.VMEM((n_deep, clip_rows, vd), BF),
            pltpu.VMEM((n_frame, clip_rows, vd), BF),
            pltpu.VMEM((clip_rows, vff), F32),
            pltpu.VMEM((n_ctx, rows, width), BF),
            pltpu.VMEM((n_ctx, 8, rows), F32),
            pltpu.VMEM((n_ctx, 8, rows), F32),
            pltpu.VMEM((n_ctx * heads, key_rows, rows), BF),
            pltpu.VMEM((key_rows, width), F32),
            pltpu.VMEM((key_rows, width), F32),
            pltpu.VMEM((n_ctx, width, rows), BF),
            pltpu.SemaphoreType.DMA((7, n_ctx)),
            pltpu.SemaphoreType.DMA((7, n_ctx)),
            pltpu.SemaphoreType.DMA((4, n_deep)),
            pltpu.SemaphoreType.DMA((4, n_deep)),
            pltpu.SemaphoreType.DMA((7,)),
        ],
        compiler_params=pltpu.CompilerParams(
            collective_id=0, has_side_effects=True, vmem_limit_bytes=60 * 1024 * 1024
        ),
    )
    query_grad, key_grad, value_grad, reward = call(
        queries,
        keys,
        values,
        query_frames.reshape(1, -1),
        frame_counts.reshape(1, -1),
        clip_of_frame.reshape(1, -1),
        cosines,
        sines,
        in_proj,
        mlp_up,
        mlp_down,
        reward_head.reshape(1, -1),
    )
    query_grad, key_grad, value_grad = deliver(query_grad, key_grad, value_grad)
    return query_grad, key_grad, value_grad, reward.reshape(1)


def solution(mesh):
    return jax.shard_map(
        functools.partial(shards, mesh.shape["ctx"], mesh.shape["frame"]),
        mesh=mesh,
        in_specs=(
            P("ctx", "frame"),
            P("ctx", "frame"),
            P("ctx", "frame"),
            P("ctx"),
            P(),
            P("ctx"),
            P("frame", None),
            P(),
            P(),
            P(),
        ),
        out_specs=(P("ctx", "frame"), P("ctx", "frame"), P("ctx", "frame"), P(("ctx", "frame"))),
        check_vma=False,
    )
```

```python
import functools
import math

import jax
import jax.numpy as jnp
import numpy as np
from jax import lax
from jax.experimental import pallas as pl
from jax.experimental.pallas import tpu as pltpu
from jax.sharding import PartitionSpec as P

HD = 128
FTOK = 16
CLIP = 2
EPSILON = 1e-05
NEG = -1e30
LOG2E = math.log2(math.e)
MESH = pl.DeviceIdType.MESH
BF = jnp.bfloat16
F32 = jnp.float32
VCHUNK = 512
PIECES = 4

NN = (((1,), (0,)), ((), ()))
NT = (((1,), (1,)), ((), ()))


def mm(left, right, dims):
    return lax.dot_general(left, right, dims, preferred_element_type=F32)


def iota(shape, dim):
    return lax.broadcasted_iota(jnp.int32, shape, dim)


def norm_stats(x):
    center = jnp.mean(x, axis=-1, keepdims=True)
    centered = x - center
    inverse = lax.rsqrt(jnp.mean(centered * centered, axis=-1, keepdims=True) + EPSILON)
    return centered * inverse, inverse


def norm_back(grad, hat, inverse):
    return inverse * (
        grad
        - jnp.mean(grad, axis=-1, keepdims=True)
        - hat * jnp.mean(grad * hat, axis=-1, keepdims=True)
    )


def kernel(
    n_ctx,
    n_frame,
    q_ref,
    k_ref,
    v_ref,
    qf_ref,
    fc_ref,
    cf_ref,
    cos_ref,
    sin_ref,
    ip_ref,
    up_ref,
    down_ref,
    head_ref,
    dq_ref,
    dk_ref,
    dv_ref,
    rew_ref,
    kin,
    vin,
    ip,
    up,
    down,
    qbuf,
    krt,
    vt,
    cosk,
    sink,
    cosq,
    sinq,
    osend,
    orecv,
    ssend,
    srecv,
    ot,
    xsend,
    xpair,
    xsum,
    xrecv,
    gbuf,
    gp,
    dobuf,
    lbuf,
    sbuf,
    stash,
    dkacc,
    dvacc,
    dqrecv,
    csend,
    crecv,
    fsend,
    frecv,
    local,
):
    me = lax.axis_index("ctx")
    fi = lax.axis_index("frame")
    rows, width = q_ref.shape
    key_rows = k_ref.shape[0]
    heads = width // HD
    slots = qf_ref.shape[1]
    clip_rows = CLIP * FTOK
    vd = ip_ref.shape[1]
    vff = up_ref.shape[1]
    key_frames = key_rows // FTOK
    scale = 1.0 / math.sqrt(HD)
    n_deep = n_frame // 2
    core, deep = lax.rem(fi, 2), lax.div(fi, 2)
    sibling = fi + 1 - 2 * core

    def deep_peer(d):
        return lax.rem(deep + d, n_deep) * 2 + core

    loads = [
        pltpu.make_async_copy(src, dst, local.at[i])
        for i, (src, dst) in enumerate(
            [(k_ref, kin), (v_ref, vin), (ip_ref, ip), (up_ref, up), (down_ref, down)]
        )
    ]
    for load in loads:
        load.start()

    barrier = pltpu.get_barrier_semaphore()
    for d in range(1, n_ctx):
        pl.semaphore_signal(
            barrier, inc=1, device_id={"ctx": lax.rem(me + d, n_ctx)}, device_id_type=MESH
        )
    for peer in [sibling] + [deep_peer(d) for d in range(1, n_deep)]:
        pl.semaphore_signal(barrier, inc=1, device_id={"frame": peer}, device_id_type=MESH)

    def send_ctx(phase, src, dst, offset, index):
        return pltpu.make_async_remote_copy(
            src_ref=src,
            dst_ref=dst,
            send_sem=csend.at[phase, index],
            recv_sem=crecv.at[phase, offset],
            device_id={"ctx": lax.rem(me + offset, n_ctx)},
            device_id_type=MESH,
        )

    def send_frame(phase, src, dst, peer, d):
        return pltpu.make_async_remote_copy(
            src_ref=src,
            dst_ref=dst,
            send_sem=fsend.at[phase, d],
            recv_sem=frecv.at[phase, d],
            device_id={"frame": peer},
            device_id_type=MESH,
        )

    def table(cos_a, sin_a, cos_b, sin_b):
        n_a = cos_a.shape[0]
        cos_a, sin_a = cos_a[:, None, :], sin_a[:, None, :]
        cos_b, sin_b = cos_b[None], sin_b[None]
        return (
            (cos_a * cos_b - sin_a * sin_b).reshape(n_a * FTOK, HD),
            (sin_a * cos_b + cos_a * sin_b).reshape(n_a * FTOK, HD),
        )

    all_frames = cos_ref.shape[0] - FTOK
    cos_t, sin_t = cos_ref[all_frames:, :], sin_ref[all_frames:, :]
    eye = iota((slots, slots), 0) == iota((slots, slots), 1)
    frame_col = jnp.sum(jnp.where(eye, qf_ref[...].astype(F32), 0.0), axis=1, keepdims=True)
    choose = jnp.where(iota((slots, all_frames), 1).astype(F32) == frame_col, 1.0, 0.0)

    def chosen(ref):
        return lax.dot_general(
            choose,
            ref[:all_frames, :],
            NN,
            precision=lax.Precision.HIGHEST,
            preferred_element_type=F32,
        )

    cos_q, sin_q = table(chosen(cos_ref), chosen(sin_ref), cos_t, sin_t)
    cosq[...] = cos_q
    sinq[...] = sin_q
    for h in range(heads):
        part = q_ref[:, h * HD : (h + 1) * HD].astype(F32)
        qbuf[0, :, h * HD : (h + 1) * HD] = (
            part * cos_q + pltpu.roll(part, HD // 2, 1) * sin_q
        ).astype(BF)

    pl.semaphore_wait(barrier, n_ctx - 1 + n_deep)
    q_sends = [send_ctx(0, qbuf.at[0], qbuf.at[d], d, d) for d in range(1, n_ctx)]
    for copy in q_sends:
        copy.start()

    own_frames = pl.ds(pl.multiple_of(me * key_frames, 8), key_frames)
    cos_k, sin_k = table(cos_ref[own_frames, :], sin_ref[own_frames, :], cos_t, sin_t)
    cosk[...] = cos_k
    sink[...] = sin_k
    loads[0].wait()
    loads[1].wait()
    for h in range(heads):
        part = kin[:, h * HD : (h + 1) * HD].astype(F32)
        turned = (part * cosk[...] + pltpu.roll(part, HD // 2, 1) * sink[...]).astype(BF)
        kin[:, h * HD : (h + 1) * HD] = turned
        krt[h * HD : (h + 1) * HD, :] = turned.astype(F32).T.astype(BF)
        vt[h * HD : (h + 1) * HD, :] = vin[:, h * HD : (h + 1) * HD].astype(F32).T.astype(BF)

    live_total = jnp.sum(fc_ref[...].astype(F32), axis=1, keepdims=True)
    key_at = (iota((key_rows, 1), 0) + me * key_rows).astype(F32)
    bias = jnp.where(key_at < live_total, 0.0, NEG)

    def forward(d, out_ref, stat_ref):
        for h in range(heads):
            cols = slice(h * HD, (h + 1) * HD)
            s = mm(kin[:, cols], qbuf[d, :, cols], NT) * (scale * LOG2E) + bias
            top = jnp.max(s, axis=0, keepdims=True)
            p = jnp.exp2(s - top)
            total = jnp.sum(p, axis=0, keepdims=True)
            o = mm(vt[cols, :], p.astype(BF), NN) * (1.0 / total)
            out_ref[cols, :] = o.astype(BF)
            stat_ref[h : h + 1, :] = top + jnp.log2(total)

    ssend[...] = jnp.zeros_like(ssend)
    forward(0, orecv.at[0], srecv.at[0])

    def o_copies(d):
        back = n_ctx - d
        return (
            send_ctx(1, osend.at[d], orecv.at[back], back, d),
            send_ctx(2, ssend.at[d], srecv.at[back], back, d),
        )

    @pl.loop(1, n_ctx)
    def _(d):
        send_ctx(0, qbuf.at[0], qbuf.at[d], d, d).wait_recv()
        forward(d, osend.at[d], ssend.at[d])
        for copy in o_copies(d):
            copy.start()

    clip_row = cf_ref[...].astype(F32)
    clip_col = jnp.sum(jnp.where(eye, clip_row, 0.0), axis=1, keepdims=True)
    earlier = jnp.logical_and(
        clip_col == clip_row, iota((slots, slots), 1) < iota((slots, slots), 0)
    )
    dest_col = clip_col * CLIP + jnp.sum(jnp.where(earlier, 1.0, 0.0), axis=1, keepdims=True)
    dest_row = jnp.sum(jnp.where(eye, dest_col, 0.0), axis=0, keepdims=True)
    wide_row = (
        jnp.sum(
            jnp.where(iota((slots, rows), 0) == lax.div(iota((slots, rows), 1), FTOK), dest_col, 0.0),
            axis=0,
            keepdims=True,
        )
        * FTOK
        + lax.rem(iota((1, rows), 1), FTOK).astype(F32)
    )
    wide_col = (
        jnp.sum(
            jnp.where(lax.div(iota((rows, slots), 0), FTOK) == iota((rows, slots), 1), dest_row, 0.0),
            axis=1,
            keepdims=True,
        )
        * FTOK
        + lax.rem(iota((rows, 1), 0), FTOK).astype(F32)
    )
    to_group = jnp.where(iota((rows, rows), 0).astype(F32) == wide_row, 1.0, 0.0).astype(BF)
    from_group = jnp.where(iota((rows, rows), 1).astype(F32) == wide_col, 1.0, 0.0).astype(BF)
    count_col = jnp.clip(live_total - frame_col * FTOK, 0.0, float(FTOK))
    live = jnp.zeros((clip_rows, 1), F32)
    count = jnp.zeros((1, 1), F32)
    for j in range(CLIP):
        mine = (fi * CLIP + j).astype(F32)
        tokens = jnp.sum(jnp.where(dest_col == mine, count_col, 0.0), axis=0, keepdims=True)
        at = (iota((clip_rows, 1), 0) - j * FTOK).astype(F32)
        live = live + jnp.where(jnp.logical_and(at >= 0.0, at < tokens), 1.0, 0.0)
        count = count + tokens

    loads[2].wait()
    for d in range(1, n_ctx):
        send_ctx(1, osend.at[d], orecv.at[d], d, d).wait_recv()
        send_ctx(2, ssend.at[d], srecv.at[d], d, d).wait_recv()
    lbuf[0] = jnp.zeros_like(lbuf[0])
    sbuf[0] = jnp.zeros_like(sbuf[0])
    for h in range(heads):
        cols = slice(h * HD, (h + 1) * HD)
        logs = [srecv[c, h : h + 1, :] for c in range(n_ctx)]
        top = functools.reduce(jnp.maximum, logs)
        shares = [jnp.exp2(x - top) for x in logs]
        total = functools.reduce(jnp.add, shares)
        inverse = 1.0 / total
        acc = jnp.zeros((HD, rows), F32)
        for c in range(n_ctx):
            acc = acc + orecv[c, cols, :].astype(F32) * (shares[c] * inverse)
        ot[cols, :] = acc.astype(BF)
        lbuf[0, h : h + 1, :] = top + jnp.log2(total)
    l_sends = [send_ctx(6, lbuf.at[0], lbuf.at[d], d, d) for d in range(1, n_ctx)]
    for copy in l_sends:
        copy.start()

    grouped = mm(to_group, ot[...], NT).astype(BF)
    shares = mm(grouped, ip[...], NN).astype(BF)
    for f in range(n_frame):
        xsend[f % 2, f // 2] = shares[f * clip_rows : (f + 1) * clip_rows, :]
    pair_send = send_frame(3, xsend.at[1 - core], xpair, sibling, 0)
    pair_send.start()
    pair_send.wait_recv()
    xsum[...] = (xsend[core].astype(F32) + xpair[...].astype(F32)).astype(BF)
    x_sends = [
        send_frame(0, xsum.at[lax.rem(deep + d, n_deep)], xrecv.at[d], deep_peer(d), d)
        for d in range(1, n_deep)
    ]
    for copy in x_sends:
        copy.start()

    def keep_weights(d):
        for h in range(heads):
            cols = slice(h * HD, (h + 1) * HD)
            s = mm(kin[:, cols], qbuf[d, :, cols], NT) * (scale * LOG2E) + bias
            stash[d * heads + h] = jnp.exp2(s - lbuf[d, h : h + 1, :]).astype(BF)

    keep_weights(0)

    @pl.loop(1, n_ctx)
    def _(d):
        send_ctx(6, lbuf.at[0], lbuf.at[d], d, d).wait_recv()
        keep_weights(d)

    x = xsend[core, deep].astype(F32) + xpair[deep].astype(F32)
    for d in range(1, n_deep):
        x_sends[d - 1].wait_recv()
        x = x + xrecv[d].astype(F32)

    hat, inverse = norm_stats(x)
    y = hat.astype(BF)
    loads[3].wait()
    loads[4].wait()
    c0 = math.sqrt(2.0 / math.pi)
    c1 = 0.044715

    def mlp_step(j, hidden):
        cols = pl.ds(pl.multiple_of(j * VCHUNK, VCHUNK), VCHUNK)
        u = mm(y, up[:, cols], NN)
        t = jnp.tanh(c0 * (u + c1 * u * u * u))
        e = (0.5 * u * (1.0 + t)).astype(BF)
        gp[:, cols] = 0.5 * (1.0 + t) + 0.5 * u * (1.0 - t * t) * (c0 * (1.0 + 3.0 * c1 * u * u))
        return hidden + mm(e, down[cols, :], NN)

    hidden = lax.fori_loop(0, vff // VCHUNK, mlp_step, jnp.zeros((clip_rows, vd), F32))
    pooled = jnp.sum(hidden * live, axis=0, keepdims=True) / count
    pooled_hat, pooled_inverse = norm_stats(pooled)
    weight = head_ref[...]
    rew_ref[...] = count * jnp.sum(pooled_hat * weight, axis=1, keepdims=True)
    d_hidden = norm_back(weight, pooled_hat, pooled_inverse)
    high = d_hidden.astype(BF).astype(F32)
    pick = iota((16, vd), 0)
    pair = jnp.where(
        pick == 0, high, jnp.where(pick == 1, d_hidden - high, 0.0)
    ).astype(BF)

    def back_step(j, d_y):
        cols = pl.ds(pl.multiple_of(j * VCHUNK, VCHUNK), VCHUNK)
        both = mm(pair, down[cols, :], NT)
        d_e = both[0:1, :] + both[1:2, :]
        d_u = (live * d_e * gp[:, cols]).astype(BF)
        return d_y + mm(d_u, up[:, cols], NT)

    d_y = lax.fori_loop(0, vff // VCHUNK, back_step, jnp.zeros((clip_rows, vd), F32))
    gbuf[fi] = norm_back(d_y, hat, inverse).astype(BF)
    g_sends = [send_frame(1, gbuf.at[fi], gbuf.at[fi], deep_peer(d), d) for d in range(1, n_deep)]
    g_sends.append(send_frame(2, gbuf.at[fi], gbuf.at[fi], sibling, 0))
    for copy in g_sends:
        copy.start()
    for d in range(1, n_deep):
        source = deep_peer(n_deep - d)
        send_frame(1, gbuf.at[source], gbuf.at[source], deep_peer(d), d).wait_recv()
        forward_copy = send_frame(2, gbuf.at[source], gbuf.at[source], sibling, d)
        forward_copy.start()
        g_sends.append(forward_copy)
    for d in range(n_deep):
        source = lax.rem(deep + n_deep - d, n_deep) * 2 + 1 - core
        send_frame(2, gbuf.at[source], gbuf.at[source], sibling, d).wait_recv()
    g = gbuf[...].reshape(rows, vd)
    grouped_grad = mm(g, ip[...], NT).astype(BF)
    out_grad = mm(from_group, grouped_grad, NN)
    dobuf[0] = out_grad.astype(BF)
    for h in range(heads):
        cols = slice(h * HD, (h + 1) * HD)
        turned = out_grad[:, cols].T
        sbuf[0, h : h + 1, :] = jnp.sum(
            turned * ot[cols, :].astype(F32), axis=0, keepdims=True
        )
    do_sends = []
    for d in range(1, n_ctx):
        do_sends.append(send_ctx(3, dobuf.at[0], dobuf.at[d], d, d))
        do_sends.append(send_ctx(4, sbuf.at[0], sbuf.at[d], d, d))
    for copy in do_sends:
        copy.start()

    def backward(d, out_ref, first):
        for h in range(heads):
            cols = slice(h * HD, (h + 1) * HD)
            q_head = qbuf[d, :, cols]
            do_head = dobuf[d, :, cols]
            p = stash[d * heads + h]
            dp = mm(vin[:, cols], do_head, NT)
            ds = (p.astype(F32) * (dp - sbuf[d, h : h + 1, :]) * scale).astype(BF)
            dv = mm(p, do_head, NN)
            dk = mm(ds, q_head, NN)
            if first:
                dvacc[:, cols] = dv
                dkacc[:, cols] = dk
            else:
                dvacc[:, cols] = dvacc[:, cols] + dv
                dkacc[:, cols] = dkacc[:, cols] + dk
            out_ref[cols, :] = mm(krt[cols, :], ds, NN).astype(BF)

    for d in range(1, n_ctx):
        for copy in o_copies(d):
            copy.wait_send()
    backward(0, dqrecv.at[0], True)

    def dq_copy(d):
        back = n_ctx - d
        return send_ctx(5, osend.at[d], dqrecv.at[back], back, d)

    @pl.loop(1, n_ctx)
    def _(d):
        send_ctx(3, dobuf.at[0], dobuf.at[d], d, d).wait_recv()
        send_ctx(4, sbuf.at[0], sbuf.at[d], d, d).wait_recv()
        backward(d, osend.at[d], False)
        dq_copy(d).start()

    dv_store = pltpu.make_async_copy(dvacc, dv_ref, local.at[5])
    dv_store.start()
    for h in range(heads):
        cols = slice(h * HD, (h + 1) * HD)
        part = dkacc[:, cols]
        dkacc[:, cols] = part * cosk[...] - pltpu.roll(part, HD // 2, 1) * sink[...]

    dk_store = pltpu.make_async_copy(dkacc, dk_ref, local.at[6])
    dk_store.start()
    for d in range(1, n_ctx):
        send_ctx(5, osend.at[d], dqrecv.at[d], d, d).wait_recv()
    for h in range(heads):
        cols = slice(h * HD, (h + 1) * HD)
        acc = dqrecv[0, cols, :].astype(F32)
        for c in range(1, n_ctx):
            acc = acc + dqrecv[c, cols, :].astype(F32)
        part = acc.T
        dq_ref[:, cols] = part * cosq[...] - pltpu.roll(part, HD // 2, 1) * sinq[...]

    for copy in q_sends + l_sends + [pair_send] + x_sends + g_sends + do_sends:
        copy.wait_send()
    dv_store.wait()
    dk_store.wait()
    for d in range(1, n_ctx):
        dq_copy(d).wait_send()


def deliver_kernel(*refs):
    count = (len(refs) - 2) // 3
    held, sem_in, sem_out = refs[2 * count : 3 * count], refs[-2], refs[-1]
    inward, outward = [], []
    for i in range(count):
        step = refs[i].shape[0] // PIECES
        for j in range(PIECES):
            part = pl.ds(j * step, step)
            n = i * PIECES + j
            inward.append(
                pltpu.make_async_copy(refs[i].at[part], held[i].at[part], sem_in.at[n])
            )
            outward.append(
                pltpu.make_async_copy(held[i].at[part], refs[count + i].at[part], sem_out.at[n])
            )
    for copy in inward:
        copy.start()
    for arrive, leave in zip(inward, outward):
        arrive.wait()
        leave.start()
    for copy in outward:
        copy.wait()


def deliver(*arrays):
    hbm = pl.BlockSpec(memory_space=pl.ANY)
    copies = len(arrays) * PIECES
    return pl.pallas_call(
        deliver_kernel,
        out_shape=tuple(jax.ShapeDtypeStruct(a.shape, a.dtype) for a in arrays),
        in_specs=[hbm] * len(arrays),
        out_specs=(hbm,) * len(arrays),
        scratch_shapes=[pltpu.VMEM(a.shape, a.dtype) for a in arrays]
        + [pltpu.SemaphoreType.DMA((copies,)), pltpu.SemaphoreType.DMA((copies,))],
        compiler_params=pltpu.CompilerParams(vmem_limit_bytes=60 * 1024 * 1024),
    )(*arrays)


def shards(
    n_ctx,
    n_frame,
    queries,
    keys,
    values,
    query_frames,
    frame_counts,
    clip_of_frame,
    in_proj,
    mlp_up,
    mlp_down,
    reward_head,
):
    rows, width = queries.shape
    key_rows = keys.shape[0]
    vd, vff = mlp_up.shape
    half = HD // 2
    heads = width // HD
    n_deep = n_frame // 2
    clip_rows = CLIP * FTOK
    lane = np.arange(HD) % half
    frequency = np.exp(-math.log(10000.0) * lane / half).astype(np.float32)
    sign = np.where(np.arange(HD) < half, -1.0, 1.0)

    position = np.concatenate([np.arange(frame_counts.shape[0]) * FTOK, np.arange(FTOK)])
    angle = (position.astype(np.float32)[:, None] * frequency[None, :]).astype(np.float64)
    cosines = jnp.asarray(np.cos(angle).astype(np.float32))
    sines = jnp.asarray((np.sin(angle) * sign[None, :]).astype(np.float32))

    vmem = pl.BlockSpec(memory_space=pltpu.VMEM)
    hbm = pl.BlockSpec(memory_space=pl.ANY)
    call = pl.pallas_call(
        functools.partial(kernel, n_ctx, n_frame),
        out_shape=(
            jax.ShapeDtypeStruct((rows, width), F32),
            jax.ShapeDtypeStruct((key_rows, width), F32),
            jax.ShapeDtypeStruct((key_rows, width), F32),
            jax.ShapeDtypeStruct((1, 1), F32),
        ),
        in_specs=[vmem, hbm, hbm] + [vmem] * 5 + [hbm] * 3 + [vmem],
        out_specs=(vmem, hbm, hbm, vmem),
        scratch_shapes=[
            pltpu.VMEM((key_rows, width), BF),
            pltpu.VMEM((key_rows, width), BF),
            pltpu.VMEM((width, vd), BF),
            pltpu.VMEM((vd, vff), BF),
            pltpu.VMEM((vff, vd), BF),
            pltpu.VMEM((n_ctx, rows, width), BF),
            pltpu.VMEM((width, key_rows), BF),
            pltpu.VMEM((width, key_rows), BF),
            pltpu.VMEM((key_rows, HD), F32),
            pltpu.VMEM((key_rows, HD), F32),
            pltpu.VMEM((rows, HD), F32),
            pltpu.VMEM((rows, HD), F32),
            pltpu.VMEM((n_ctx, width, rows), BF),
            pltpu.VMEM((n_ctx, width, rows), BF),
            pltpu.VMEM((n_ctx, 8, rows), F32),
            pltpu.VMEM((n_ctx, 8, rows), F32),
            pltpu.VMEM((width, rows), BF),
            pltpu.VMEM((2, n_deep, clip_rows, vd), BF),
            pltpu.VMEM((n_deep, clip_rows, vd), BF),
            pltpu.VMEM((n_deep, clip_rows, vd), BF),
            pltpu.VMEM((n_deep, clip_rows, vd), BF),
            pltpu.VMEM((n_frame, clip_rows, vd), BF),
            pltpu.VMEM((clip_rows, vff), F32),
            pltpu.VMEM((n_ctx, rows, width), BF),
            pltpu.VMEM((n_ctx, 8, rows), F32),
            pltpu.VMEM((n_ctx, 8, rows), F32),
            pltpu.VMEM((n_ctx * heads, key_rows, rows), BF),
            pltpu.VMEM((key_rows, width), F32),
            pltpu.VMEM((key_rows, width), F32),
            pltpu.VMEM((n_ctx, width, rows), BF),
            pltpu.SemaphoreType.DMA((7, n_ctx)),
            pltpu.SemaphoreType.DMA((7, n_ctx)),
            pltpu.SemaphoreType.DMA((4, n_deep)),
            pltpu.SemaphoreType.DMA((4, n_deep)),
            pltpu.SemaphoreType.DMA((7,)),
        ],
        compiler_params=pltpu.CompilerParams(
            collective_id=0, has_side_effects=True, vmem_limit_bytes=60 * 1024 * 1024
        ),
    )
    query_grad, key_grad, value_grad, reward = call(
        queries,
        keys,
        values,
        query_frames.reshape(1, -1),
        frame_counts.reshape(1, -1),
        clip_of_frame.reshape(1, -1),
        cosines,
        sines,
        in_proj,
        mlp_up,
        mlp_down,
        reward_head.reshape(1, -1),
    )
    query_grad, key_grad, value_grad = deliver(query_grad, key_grad, value_grad)
    return query_grad, key_grad, value_grad, reward.reshape(1)


def solution(mesh):
    return jax.shard_map(
        functools.partial(shards, mesh.shape["ctx"], mesh.shape["frame"]),
        mesh=mesh,
        in_specs=(
            P("ctx", "frame"),
            P("ctx", "frame"),
            P("ctx", "frame"),
            P("ctx"),
            P(),
            P("ctx"),
            P("frame", None),
            P(),
            P(),
            P(),
        ),
        out_specs=(P("ctx", "frame"), P("ctx", "frame"), P("ctx", "frame"), P(("ctx", "frame"))),
        check_vma=False,
    )
```
